256 devices in a mesh: section: 8 (over z_lo, x), seq: 32 (over z_hi, y, core).
Axes of the slice: x: 4, y: 4, z: 8 (z_hi: 4, z_lo: 2; z = z_hi * 2 + z_lo), core: 2. Of those that a mesh axis runs over, the one named last changes fastest.
Arguments:
- queries: bfloat16 [8, 3072, 4096], P('section', 'seq'), may hold values from -120 to 120
- keys: bfloat16 [8, 3072, 4096], P('section', 'seq'), may hold values from -120 to 120
- values: bfloat16 [8, 3072, 4096], P('section', 'seq'), may hold values from -6 to 6
- norm_gains: float32 [2, 4096], replicated, may hold values from 1.2 to 2.5
Outputs:
- attended: bfloat16 [8, 3072, 4096], P('section', 'seq')
The draws below stay inside these ranges and needn't reach their ends.
All inputs are finite; a program needn't handle non-finite values.
Results may differ from the reference program's by a relative error of at most 0.0014.
The reference program's roundings to bfloat16 on the way count: a program that leaves them out, or rounds other values in their place, can miss the bound.
Values may be sent and summed in bfloat16 or wider, within the bound.
No kernel may reach another device: no remote copies, remote signals or barrier semaphores. Data moves between devices by JAX's collectives and lax.ppermute only.
A program may use at most 128 MiB of HBM per device.

```python
import math
import jax
import jax.numpy as jnp
from jax import lax

HEAD_DIM = 128
HEADS = 32
GROUP = 3072
SECTIONS = 8


def scaled_base(key, row_lo, row_hi):
    shape = (SECTIONS, GROUP, HEADS * HEAD_DIM)
    base = jnp.clip(jax.random.normal(jax.random.fold_in(key, 1), shape, jnp.float32), -6.0, 6.0)
    row_scale = jnp.exp(jax.random.uniform(jax.random.fold_in(key, 2), (SECTIONS, GROUP, 1), jnp.float32, jnp.log(row_lo), jnp.log(row_hi)))
    col_scale = jnp.exp(jax.random.uniform(jax.random.fold_in(key, 4), (HEADS * HEAD_DIM,), jnp.float32, jnp.log(0.4), jnp.log(4.0)))
    return base * row_scale * col_scale


def draw_queries(key, part):
    key = jax.random.fold_in(key, 3)
    result = scaled_base(key, 0.5, 5.0)
    return result.astype(jnp.bfloat16)


def draw_keys(key, part):
    key = jax.random.fold_in(key, 5)
    result = scaled_base(key, 0.5, 5.0)
    return result.astype(jnp.bfloat16)


def shard_levels(stream_key, shape, cuts, least, top_value):
    loudness, own = 1.0, jax.random.fold_in(stream_key, 6)
    for position, blocks in cuts:
        steps = jnp.exp(jax.random.uniform(jax.random.fold_in(own, position), (blocks,), jnp.float32, least / len(cuts), top_value / len(cuts)))
        loudness = loudness * jnp.repeat(steps, shape[position] // blocks).reshape([-1 if axis == position else 1 for axis in range(len(shape))])
    return loudness


def noise(own_key, dims, scale, reach, pieces=(), kind=jnp.bfloat16):
    loudness = shard_levels(own_key, dims, pieces, -0.22, 0.18) if pieces else 1.0
    values = jax.random.normal(own_key, dims, jnp.float32) * scale * loudness
    return jnp.minimum(jnp.maximum(values, -reach), reach).astype(kind)


def setup_inputs(seed: int = 0) -> dict:
    key_list = jax.random.split(jax.random.key(seed), 5)
    return {
        "queries": draw_queries(jax.random.fold_in(key_list[4], 71), 0),
        "keys": draw_keys(jax.random.fold_in(key_list[4], 71), 0),
        "values": noise(key_list[2], (SECTIONS, GROUP, HEADS * HEAD_DIM), 1.0, 6.0, ((0, 8), (1, 32))),
        "norm_gains": jnp.clip(jnp.exp(jax.random.uniform(key_list[3], (2, HEADS * HEAD_DIM), jnp.float32, math.log(1.2), math.log(2.5))), 1.2, 2.5),
    }


def normalize(rows, gain):
    wide = rows.astype(jnp.float32)
    power = lax.optimization_barrier(jnp.mean(wide * wide, axis=-1, keepdims=True))
    return (wide * lax.rsqrt(power + 1e-06) * gain).astype(jnp.bfloat16)

def attend_head(triple):
    query_head, key_head, value_head = triple
    scores = jnp.dot(query_head.astype(jnp.float32), key_head.astype(jnp.float32).T, precision=lax.Precision.HIGHEST) * (1.0 / math.sqrt(HEAD_DIM))
    rowmax = lax.optimization_barrier(jnp.max(scores, axis=1, keepdims=True))
    expo = jnp.exp(scores - rowmax)
    total = lax.optimization_barrier(jnp.sum(expo, axis=1, keepdims=True))
    weights = expo.astype(jnp.bfloat16)
    mixed = jnp.dot(weights, value_head, preferred_element_type=jnp.float32)
    return (mixed / total).astype(jnp.bfloat16)

def by_heads(rows):
    return rows.reshape(GROUP, HEADS, HEAD_DIM).transpose(1, 0, 2)

def reference(queries, keys, values, norm_gains):
    results = []
    prior_keys = None
    prior_values = None
    for section_index in range(SECTIONS):
        head_queries = by_heads(normalize(queries[section_index], norm_gains[0]))
        head_keys = by_heads(normalize(keys[section_index], norm_gains[1]))
        head_values = by_heads(values[section_index])
        if prior_keys is None:
            all_keys, all_values = (head_keys, head_values)
        else:
            all_keys = jnp.concatenate([head_keys, prior_keys], axis=1)
            all_values = jnp.concatenate([head_values, prior_values], axis=1)
        mixed = lax.map(attend_head, (head_queries, all_keys, all_values))
        results.append(mixed.transpose(1, 0, 2).reshape(GROUP, HEADS * HEAD_DIM))
        prior_keys, prior_values = (head_keys, head_values)
    return jnp.stack(results)
```

```python
import math

import jax
import jax.numpy as jnp
from jax import lax
from jax.experimental import pallas as pl
from jax.experimental.pallas import tpu as pltpu
from jax.sharding import PartitionSpec as P

HEAD_DIM = 128
EXPONENT_SCALE = math.log2(math.e) / math.sqrt(HEAD_DIM)
F32 = jnp.float32
BF16 = jnp.bfloat16
VMEM_LIMIT = 60 * 2**20
LAST_WITH_LAST = (((1,), (1,)), ((), ()))


def norm_rows(rows, gain):
    wide = rows.astype(F32)
    power = jnp.mean(wide * wide, axis=-1, keepdims=True)
    return (wide * lax.rsqrt(power + 1e-06) * gain).astype(BF16)


def split_heads(rows, chips, width):
    return [rows[:, c * width : (c + 1) * width] for c in range(chips)]


def prepare_keys_values(keys, values, gains, chips, heads):
    tokens, features = keys.shape

    def kernel(key_ref, value_ref, gain_ref, *out_refs):
        normed = norm_rows(key_ref[...], gain_ref[1:2, :])
        for h in range(heads):
            for c in range(chips):
                lo = (c * heads + h) * HEAD_DIM
                out_refs[h][c, 0] = normed[:, lo : lo + HEAD_DIM]
                out_refs[h][c, 1] = value_ref[:, lo : lo + HEAD_DIM]

    vmem = pl.BlockSpec(memory_space=pltpu.VMEM)
    return pl.pallas_call(
        kernel,
        in_specs=[vmem] * 3,
        out_specs=[vmem] * heads,
        out_shape=[jax.ShapeDtypeStruct((chips, 2, tokens, HEAD_DIM), BF16)] * heads,
        compiler_params=pltpu.CompilerParams(vmem_limit_bytes=VMEM_LIMIT),
        name="prepare_kv",
    )(keys, values, gains)


def prepare_queries(queries, gains, chips, heads):
    tokens, features = queries.shape

    def kernel(query_ref, gain_ref, out_ref):
        normed = norm_rows(query_ref[...], gain_ref[0:1, :])
        for c in range(chips):
            for h in range(heads):
                lo = (c * heads + h) * HEAD_DIM
                out_ref[c, h] = normed[:, lo : lo + HEAD_DIM]

    vmem = pl.BlockSpec(memory_space=pltpu.VMEM)
    return pl.pallas_call(
        kernel,
        in_specs=[vmem] * 2,
        out_specs=vmem,
        out_shape=jax.ShapeDtypeStruct((chips, heads, tokens, HEAD_DIM), BF16),
        compiler_params=pltpu.CompilerParams(vmem_limit_bytes=VMEM_LIMIT),
        name="prepare_q",
    )(queries, gains)


def attend(has_prior, queries, head, pieces, earlier_out, rows_block=256, keys_block=512):
    chips, heads, tokens, _ = queries.shape
    length = chips * tokens
    blocks = length // rows_block
    keys_each = length
    per = keys_each // keys_block
    cost = pl.CostEstimate(
        flops=4 * length * 4 * keys_each * HEAD_DIM,
        bytes_accessed=2 * 10 * length * HEAD_DIM,
        transcendentals=4 * length * keys_each,
    )

    def kernel(prior_ref, query_ref, *refs):
        kv = refs[:4]
        out_ref = refs[-7]
        query_rows, out_rows, scores_a, scores_b, top_a, top_b = refs[-6:]

        def piece(c, which):
            b, t = divmod(c, per)
            rows = kv[b][:, which].reshape(keys_each, HEAD_DIM)
            return rows[t * keys_block : (t + 1) * keys_block]

        def phase(ahead, behind, count):
            if ahead:
                ahead_scores, ahead_top, block = ahead
                query = query_rows[pl.ds(block * rows_block, rows_block), :]
                top = None
            if behind:
                behind_scores, behind_top, block_out = behind
                shift = jnp.max(behind_top[...], axis=1, keepdims=True) * EXPONENT_SCALE
                shift = jnp.broadcast_to(shift, (rows_block, HEAD_DIM))
                total = None
                mixed = None
            for c in range(count):
                base = c * keys_block
                if ahead:
                    raw = lax.dot_general(
                        query, piece(c, 0), LAST_WITH_LAST, preferred_element_type=F32
                    )
                    ahead_scores[:, base : base + keys_block] = raw
                    for j in range(0, keys_block, 128):
                        part = raw[:, j : j + 128]
                        top = part if top is None else jnp.maximum(top, part)
                if behind:
                    weights = []
                    for j in range(base, base + keys_block, 128):
                        expo = jnp.exp2(behind_scores[:, j : j + 128] * EXPONENT_SCALE - shift)
                        total = expo if total is None else total + expo
                        weights.append(expo.astype(BF16))
                    part = jnp.dot(
                        jnp.concatenate(weights, axis=1),
                        piece(c, 1),
                        preferred_element_type=F32,
                    )
                    mixed = part if mixed is None else mixed + part
            if ahead:
                ahead_top[...] = top
            if behind:
                total = jnp.sum(total, axis=1, keepdims=True)
                out_rows[pl.ds(block_out * rows_block, rows_block), :] = (mixed / total).astype(BF16)

        def whole(count):
            a, b = (scores_a, top_a), (scores_b, top_b)
            phase(a + (0,), None, count)

            def pair(i, carry):
                phase(b + (2 * i + 1,), a + (2 * i,), count)
                phase(a + (2 * i + 2,), b + (2 * i + 1,), count)
                return carry

            lax.fori_loop(0, blocks // 2 - 1, pair, 0)
            phase(b + (blocks - 1,), a + (blocks - 2,), count)
            phase(None, b + (blocks - 1,), count)

        query_rows[...] = query_ref[:, 0].reshape(length, HEAD_DIM)

        @pl.when(prior_ref[0] > 0)
        def _():
            whole(4 * per)

        @pl.when(prior_ref[0] == 0)
        def _():
            whole(2 * per)

        out_ref[:, 0] = out_rows[...].reshape(chips, tokens, HEAD_DIM)

    one_head = pl.BlockSpec((chips, 1, tokens, HEAD_DIM), lambda i: (0, head, 0, 0))
    kv_spec = pl.BlockSpec((chips, 2, tokens, HEAD_DIM), lambda i: (0, 0, 0, 0))
    in_specs = [pl.BlockSpec(memory_space=pltpu.SMEM), one_head] + [kv_spec] * 4
    operands = [has_prior, queries, *pieces]
    aliases = {}
    if earlier_out is not None:
        in_specs.append(pl.BlockSpec(memory_space=pl.ANY))
        aliases = {len(operands): 0}
        operands.append(earlier_out)
    return pl.pallas_call(
        kernel,
        grid=(1,),
        in_specs=in_specs,
        out_specs=one_head,
        out_shape=jax.ShapeDtypeStruct(queries.shape, BF16),
        scratch_shapes=[
            pltpu.VMEM((length, HEAD_DIM), BF16),
            pltpu.VMEM((length, HEAD_DIM), BF16),
            pltpu.VMEM((rows_block, 4 * keys_each), F32),
            pltpu.VMEM((rows_block, 4 * keys_each), F32),
            pltpu.VMEM((rows_block, HEAD_DIM), F32),
            pltpu.VMEM((rows_block, HEAD_DIM), F32),
        ],
        input_output_aliases=aliases,
        cost_estimate=cost,
        compiler_params=pltpu.CompilerParams(vmem_limit_bytes=VMEM_LIMIT),
        name="attend",
    )(*operands)


def local(queries, keys, values, norm_gains):
    seq = lax.axis_size("seq")
    sections = lax.axis_size("section")
    chips = seq // 2
    tokens, features = queries.shape[1:]
    heads = features // HEAD_DIM // chips
    same_core = [[2 * p + c for p in range(chips)] for c in range(2)]

    def exchange(x):
        return lax.all_to_all(
            x, "seq", split_axis=0, concat_axis=0, tiled=True, axis_index_groups=same_core
        )

    def swap(x):
        return lax.ppermute(x, "seq", [(i, i ^ 1) for i in range(seq)])

    def passed_on(x):
        return lax.ppermute(x, "section", [(s, s + 1) for s in range(sections - 1)])

    has_prior = (lax.axis_index("section") > 0).astype(jnp.int32).reshape(1)
    sent = prepare_keys_values(keys[0], values[0], norm_gains, chips, heads)
    both = exchange(jnp.concatenate(sent, axis=1))
    own = [both[:, 2 * h : 2 * h + 2] for h in range(heads)]
    query_sent = prepare_queries(queries[0], norm_gains, chips, heads)
    query_sent, own = lax.optimization_barrier((query_sent, own))
    prior = [passed_on(x) for x in own]
    head_queries = exchange(query_sent)
    own_other = [swap(x) for x in own]
    prior_other = [swap(x) for x in prior]
    out = None
    for h in range(heads):
        pieces = (own[h], own_other[h], prior[h], prior_other[h])
        out = attend(has_prior, head_queries, h, pieces, out)
    back = exchange(out)
    return jnp.transpose(back, (2, 0, 1, 3)).reshape(1, tokens, features)


def solution(mesh):
    return jax.shard_map(
        local,
        mesh=mesh,
        in_specs=(
            P("section", "seq", None),
            P("section", "seq", None),
            P("section", "seq", None),
            P(),
        ),
        out_specs=P("section", "seq", None),
        check_vma=False,
    )
```

```python
import math

import jax
import jax.numpy as jnp
from jax import lax
from jax.experimental import pallas as pl
from jax.experimental.pallas import tpu as pltpu
from jax.sharding import PartitionSpec as P

HEAD_DIM = 128
RING = 4
CHIPS = RING * RING
EXPONENT_SCALE = math.log2(math.e) / math.sqrt(HEAD_DIM)
F32 = jnp.float32
BF16 = jnp.bfloat16
VMEM_LIMIT = 26 * 2**20
LAST_WITH_LAST = (((1,), (1,)), ((), ()))
VMEM = pl.BlockSpec(memory_space=pltpu.VMEM)
SMEM = pl.BlockSpec(memory_space=pltpu.SMEM)


def head_column(scalars, z, y, h):
    z = lax.rem(z + h * scalars[2], RING)
    return pl.multiple_of(((z * RING + y) * 2 + h) * HEAD_DIM, HEAD_DIM)


def norm_rows(rows, gain):
    wide = rows.astype(F32)
    power = jnp.mean(wide * wide, axis=-1, keepdims=True)
    return (wide * lax.rsqrt(power + 1e-06) * gain).astype(BF16)


def prepare_keys_values(scalars, keys, values, gain):
    tokens, features = keys.shape

    def kernel(scalar_ref, key_ref, value_ref, gain_ref, out_ref, normed):
        normed[...] = norm_rows(key_ref[...], gain_ref[...])
        for c in range(CHIPS):
            for h in range(2):
                column = head_column(scalar_ref, c // RING, c % RING, h)
                out_ref[c, h, 0] = normed[:, pl.ds(column, HEAD_DIM)]
                out_ref[c, h, 1] = value_ref[:, pl.ds(column, HEAD_DIM)]

    return pl.pallas_call(
        kernel,
        in_specs=[SMEM] + [VMEM] * 3,
        out_specs=VMEM,
        out_shape=jax.ShapeDtypeStruct((CHIPS, 2, 2, tokens, HEAD_DIM), BF16),
        scratch_shapes=[pltpu.VMEM((tokens, features), BF16)],
        compiler_params=pltpu.CompilerParams(vmem_limit_bytes=VMEM_LIMIT),
        name="prepare_kv",
    )(scalars, keys, values, gain)


def prepare_queries(scalars, queries, gain):
    tokens, features = queries.shape

    def kernel(scalar_ref, query_ref, gain_ref, out_ref, normed):
        normed[...] = norm_rows(query_ref[...], gain_ref[...])
        for c in range(CHIPS):
            for h in range(2):
                column = head_column(scalar_ref, c // RING, c % RING, h)
                out_ref[c, h] = normed[:, pl.ds(column, HEAD_DIM)]

    return pl.pallas_call(
        kernel,
        in_specs=[SMEM] + [VMEM] * 2,
        out_specs=VMEM,
        out_shape=jax.ShapeDtypeStruct((CHIPS, 2, tokens, HEAD_DIM), BF16),
        scratch_shapes=[pltpu.VMEM((tokens, features), BF16)],
        compiler_params=pltpu.CompilerParams(vmem_limit_bytes=VMEM_LIMIT),
        name="prepare_q",
    )(scalars, queries, gain)


def collect(scalars, blocks):
    tokens = blocks[0].shape[2]

    def kernel(scalar_ref, *refs):
        out_ref = refs[-1]
        for dy in range(RING):
            for dz in range(RING):
                for h in range(2):
                    z = lax.rem(scalar_ref[0] + (RING - dz), RING)
                    y = lax.rem(scalar_ref[1] + (RING - dy), RING)
                    column = head_column(scalar_ref, z, y, h)
                    out_ref[:, pl.ds(column, HEAD_DIM)] = refs[dy][h, dz]

    return pl.pallas_call(
        kernel,
        in_specs=[SMEM] + [VMEM] * RING,
        out_specs=VMEM,
        out_shape=jax.ShapeDtypeStruct((tokens, CHIPS * 2 * HEAD_DIM), BF16),
        compiler_params=pltpu.CompilerParams(vmem_limit_bytes=VMEM_LIMIT),
        name="collect",
    )(scalars, *blocks)


def attend(scalars, queries, h, distances, pieces, earlier=None, rows_block=192, keys_block=512):
    tokens = queries.shape[2]
    keys_each = CHIPS * tokens
    per = keys_each // keys_block
    splits = RING * tokens // rows_block
    inner = rows_block // tokens
    count_q = len(distances)
    rows_all = count_q * RING * tokens
    cost = pl.CostEstimate(
        flops=4 * rows_all * 4 * keys_each * HEAD_DIM,
        bytes_accessed=2 * 2 * 4 * keys_each * HEAD_DIM,
        transcendentals=rows_all * 4 * keys_each,
    )

    def kernel(scalar_ref, *refs):
        query_refs, refs = refs[:count_q], refs[count_q:]
        kv, refs = refs[:4], refs[4:]
        if earlier is not None:
            earlier_refs, refs = refs[:count_q], refs[count_q:]
        out_refs, (scores_a, scores_b, top_a, top_b) = refs[:count_q], refs[count_q:]

        def piece(c, which):
            b, t = divmod(c, per)
            rows = kv[b][:, 0, which] if b < 2 else kv[b][:, which]
            return rows.reshape(keys_each, HEAD_DIM)[t * keys_block : (t + 1) * keys_block]

        def away(j):
            return lax.rem(j + RING - scalar_ref[1], RING)

        def phase(ahead, behind, count):
            if ahead:
                scores_in, top_in, d_in, r_in = ahead
                query = query_refs[d_in][r_in * inner : (r_in + 1) * inner, 0]
                query = query.reshape(rows_block, HEAD_DIM)
                top = None
            if behind:
                scores_out, top_out, d_out, r_out = behind
                shift = jnp.max(top_out[...], axis=1, keepdims=True) * EXPONENT_SCALE
                shift = jnp.broadcast_to(shift, (rows_block, HEAD_DIM))
                total = None
                mixed = None
            for c in range(count):
                base = c * keys_block
                if ahead:
                    raw = lax.dot_general(
                        query, piece(c, 0), LAST_WITH_LAST, preferred_element_type=F32
                    )
                    scores_in[:, base : base + keys_block] = raw
                    for j in range(0, keys_block, 128):
                        part = raw[:, j : j + 128]
                        top = part if top is None else jnp.maximum(top, part)
                if behind:
                    weights = []
                    for j in range(base, base + keys_block, 128):
                        expo = jnp.exp2(scores_out[:, j : j + 128] * EXPONENT_SCALE - shift)
                        total = expo if total is None else total + expo
                        weights.append(expo.astype(BF16))
                    part = jnp.dot(
                        jnp.concatenate(weights, axis=1),
                        piece(c, 1),
                        preferred_element_type=F32,
                    )
                    mixed = part if mixed is None else mixed + part
            if ahead:
                top_in[...] = top
            if behind:
                total = jnp.sum(total, axis=1, keepdims=True)
                result = (mixed / total).astype(BF16)
                for j in range(inner):
                    rows = result[j * tokens : (j + 1) * tokens]
                    if earlier is None:
                        out_refs[d_out][away(r_out * inner + j)] = rows
                    else:
                        out_refs[d_out][h, away(r_out * inner + j)] = rows

        def whole(count):
            halves = [(scores_a, top_a), (scores_b, top_b)]
            jobs = [(d, r) for d in range(count_q) for r in range(splits)]
            jobs = [halves[i % 2] + job for i, job in enumerate(jobs)]
            for ahead, behind in zip(jobs + [None], [None] + jobs):
                phase(ahead, behind, count)

        if earlier is not None:
            for d in range(count_q):
                out_refs[d][0] = earlier_refs[d][...]

        @pl.when(scalar_ref[3] > 0)
        def _():
            whole(4 * per)

        @pl.when(scalar_ref[3] == 0)
        def _():
            whole(2 * per)

    def query_spec(dz):
        return pl.BlockSpec(
            (RING, 1, tokens, HEAD_DIM), lambda i, s: (lax.rem(s[0] + dz, RING), h, 0, 0)
        )

    own_spec = pl.BlockSpec((CHIPS, 1, 2, tokens, HEAD_DIM), lambda i, s: (0, h, 0, 0, 0))
    prior_spec = pl.BlockSpec((CHIPS, 2, tokens, HEAD_DIM), lambda i, s: (0, 0, 0, 0))
    one_spec = pl.BlockSpec((RING, tokens, HEAD_DIM), lambda i, s: (0, 0, 0))
    both_spec = pl.BlockSpec((2, RING, tokens, HEAD_DIM), lambda i, s: (0, 0, 0, 0))
    in_specs = [query_spec(dz) for dz in distances] + [own_spec] * 2 + [prior_spec] * 2
    operands = [queries] * count_q + list(pieces)
    out_spec, out_dims = one_spec, (RING, tokens, HEAD_DIM)
    if earlier is not None:
        in_specs += [one_spec] * count_q
        operands += earlier
        out_spec, out_dims = both_spec, (2, RING, tokens, HEAD_DIM)
    return pl.pallas_call(
        kernel,
        grid_spec=pltpu.PrefetchScalarGridSpec(
            num_scalar_prefetch=1,
            grid=(1,),
            in_specs=in_specs,
            out_specs=[out_spec] * count_q,
            scratch_shapes=[
                pltpu.VMEM((rows_block, 4 * keys_each), F32),
                pltpu.VMEM((rows_block, 4 * keys_each), F32),
                pltpu.VMEM((rows_block, HEAD_DIM), F32),
                pltpu.VMEM((rows_block, HEAD_DIM), F32),
            ],
        ),
        out_shape=[jax.ShapeDtypeStruct(out_dims, BF16)] * count_q,
        cost_estimate=cost,
        compiler_params=pltpu.CompilerParams(vmem_limit_bytes=VMEM_LIMIT),
        name="attend",
    )(scalars, *operands)


def local(queries, keys, values, norm_gains):
    seq = lax.axis_size("seq")
    sections = lax.axis_size("section")
    here = lax.axis_index("seq")
    section = lax.axis_index("section")
    late = (section >= sections // 2).astype(jnp.int32)
    has_prior = (section > 0).astype(jnp.int32)
    scalars = jnp.stack([here // 8, here % 8 // 2, late, has_prior]).astype(jnp.int32)
    same_core = [[2 * p + c for p in range(CHIPS)] for c in range(2)]
    fence = lax.optimization_barrier

    def exchange(x):
        return lax.all_to_all(
            x, "seq", split_axis=0, concat_axis=0, tiled=True, axis_index_groups=same_core
        )

    def along(x, dz, dy):
        def target(i):
            z, y, core = i // 8, i % 8 // 2, i % 2
            return (z + dz) % RING * 8 + (y + dy) % RING * 2 + core

        return lax.ppermute(x, "seq", [(i, target(i)) for i in range(seq)])

    def swap(x):
        return lax.ppermute(x, "seq", [(i, i ^ 1) for i in range(seq)])

    def passed_on(x, h):
        route = []
        for s in range(sections - 1):
            back = 8 * h if s + 1 == sections // 2 else 0
            for i in range(seq):
                route.append((s * seq + i, (s + 1) * seq + (i - back) % seq))
        return lax.ppermute(x, ("section", "seq"), route)

    own = exchange(prepare_keys_values(scalars, keys[0], values[0], norm_gains[1:2]))
    query_sent = prepare_queries(scalars, queries[0], norm_gains[0:1])
    query_sent, own = fence((query_sent, own))
    prior_a = passed_on(own[:, 0], 0)
    head_queries = exchange(query_sent)
    own_other = swap(own)
    prior_a, own_b = fence((prior_a, own[:, 1]))
    prior_b = passed_on(own_b, 1)
    prior_a_other = swap(prior_a)

    pieces = (own, own_other, prior_a, prior_a_other)
    first = attend(scalars, head_queries, 0, (2, 1), pieces)
    first, prior_b, head_queries = fence((first, prior_b, head_queries))
    prior_b_other = swap(prior_b)
    first += attend(scalars, head_queries, 0, (3, 0), pieces)

    pieces = (own, own_other, prior_b, prior_b_other)
    home_z = {}
    for dz, half in zip((2, 1, 3, 0), first):
        (mine,) = attend(scalars, head_queries, 1, (dz,), pieces, [half])
        home_z[dz] = along(mine, dz, 0) if dz else mine
    turned = [jnp.stack([home_z[dz][:, dy] for dz in range(RING)], axis=1) for dy in range(RING)]
    turned = fence(turned)
    home = [turned[0]] + [along(turned[dy], 0, dy) for dy in range(1, RING)]
    return collect(scalars, home)[None]


def solution(mesh):
    return jax.shard_map(
        local,
        mesh=mesh,
        in_specs=(
            P("section", "seq", None),
            P("section", "seq", None),
            P("section", "seq", None),
            P(),
        ),
        out_specs=P("section", "seq", None),
        check_vma=False,
    )
```

```python
import math

import jax
import jax.numpy as jnp
from jax import lax
from jax.experimental import pallas as pl
from jax.experimental.pallas import tpu as pltpu
from jax.sharding import PartitionSpec as P

HEAD_DIM = 128
RING = 4
CHIPS = RING * RING
EXPONENT_SCALE = math.log2(math.e) / math.sqrt(HEAD_DIM)
F32 = jnp.float32
BF16 = jnp.bfloat16
VMEM_LIMIT = 32 * 2**20
PREPARE_VMEM = 60 * 2**20
LAST_WITH_LAST = (((1,), (1,)), ((), ()))
VMEM = pl.BlockSpec(memory_space=pltpu.VMEM)
SMEM = pl.BlockSpec(memory_space=pltpu.SMEM)


def head_column(scalars, z, y, h):
    z = lax.rem(z + h * scalars[2], RING)
    return pl.multiple_of(((z * RING + y) * 2 + h) * HEAD_DIM, HEAD_DIM)


def norm_rows(rows, gain):
    wide = rows.astype(F32)
    power = jnp.mean(wide * wide, axis=-1, keepdims=True)
    return (wide * lax.rsqrt(power + 1e-06) * gain).astype(BF16)


def prepare_keys_values(scalars, keys, values, gain, rows_block=48):
    tokens, features = keys.shape

    def kernel(scalar_ref, key_ref, value_ref, gain_ref, out_ref, normed):
        normed[...] = norm_rows(key_ref[...], gain_ref[...])
        for c in range(CHIPS):
            for h in range(2):
                column = head_column(scalar_ref, c // RING, c % RING, h)
                out_ref[c, h, 0] = normed[:, pl.ds(column, HEAD_DIM)]
                out_ref[c, h, 1] = value_ref[:, pl.ds(column, HEAD_DIM)]

    rows_spec = pl.BlockSpec((rows_block, features), lambda i, s: (i, 0))
    return pl.pallas_call(
        kernel,
        grid_spec=pltpu.PrefetchScalarGridSpec(
            num_scalar_prefetch=1,
            grid=(tokens // rows_block,),
            in_specs=[rows_spec] * 2 + [pl.BlockSpec((1, features), lambda i, s: (0, 0))],
            out_specs=pl.BlockSpec(
                (CHIPS, 2, 2, rows_block, HEAD_DIM), lambda i, s: (0, 0, 0, i, 0)
            ),
            scratch_shapes=[pltpu.VMEM((rows_block, features), BF16)],
        ),
        out_shape=jax.ShapeDtypeStruct((CHIPS, 2, 2, tokens, HEAD_DIM), BF16),
        compiler_params=pltpu.CompilerParams(vmem_limit_bytes=PREPARE_VMEM),
        name="prepare_kv",
    )(scalars, keys, values, gain)


def prepare_queries(scalars, queries, gain):
    tokens, features = queries.shape

    def kernel(scalar_ref, query_ref, gain_ref, out_ref, normed):
        normed[...] = norm_rows(query_ref[...], gain_ref[...])
        for c in range(CHIPS):
            for h in range(2):
                column = head_column(scalar_ref, c // RING, c % RING, h)
                out_ref[c, h] = normed[:, pl.ds(column, HEAD_DIM)]

    return pl.pallas_call(
        kernel,
        in_specs=[SMEM] + [VMEM] * 2,
        out_specs=VMEM,
        out_shape=jax.ShapeDtypeStruct((CHIPS, 2, tokens, HEAD_DIM), BF16),
        scratch_shapes=[pltpu.VMEM((tokens, features), BF16)],
        compiler_params=pltpu.CompilerParams(vmem_limit_bytes=VMEM_LIMIT),
        name="prepare_q",
    )(scalars, queries, gain)


def collect(scalars, blocks):
    tokens = blocks.shape[2]

    def kernel(scalar_ref, block_ref, out_ref):
        for c in range(CHIPS):
            for h in range(2):
                column = head_column(scalar_ref, c // RING, c % RING, h)
                out_ref[:, pl.ds(column, HEAD_DIM)] = block_ref[c, h]

    return pl.pallas_call(
        kernel,
        in_specs=[SMEM, VMEM],
        out_specs=VMEM,
        out_shape=jax.ShapeDtypeStruct((tokens, CHIPS * 2 * HEAD_DIM), BF16),
        compiler_params=pltpu.CompilerParams(vmem_limit_bytes=VMEM_LIMIT),
        name="collect",
    )(scalars, blocks)


def attend(scalars, queries, pieces, rows_block=192, keys_block=512):
    tokens = queries.shape[2]
    keys_each = CHIPS * tokens
    per = keys_each // keys_block
    inner = rows_block // tokens
    blocks = CHIPS // inner
    rows_all = 2 * CHIPS * tokens
    cost = pl.CostEstimate(
        flops=4 * rows_all * 4 * keys_each * HEAD_DIM,
        bytes_accessed=2 * 2 * 2 * 4 * keys_each * HEAD_DIM,
        transcendentals=rows_all * 4 * keys_each,
    )

    def kernel(scalar_ref, query_ref, *refs):
        own, prior = refs[:2], refs[2:6]
        out_ref, scores_a, scores_b, top_a, top_b = refs[6:]

        def piece(h, c, which):
            b, t = divmod(c, per)
            rows = own[b][:, h, which] if b < 2 else prior[2 * b - 4 + h][:, which]
            return rows.reshape(keys_each, HEAD_DIM)[t * keys_block : (t + 1) * keys_block]

        def phase(ahead, behind, count):
            if ahead:
                scores_in, top_in, h_in, r_in = ahead
                query = jnp.concatenate(
                    [query_ref[r_in * inner + j, h_in] for j in range(inner)], axis=0
                )
                top = None
            if behind:
                scores_out, top_out, h_out, r_out = behind
                shift = jnp.max(top_out[...], axis=1, keepdims=True) * EXPONENT_SCALE
                shift = jnp.broadcast_to(shift, (rows_block, HEAD_DIM))
                total = None
                mixed = None
            for c in range(count):
                base = c * keys_block
                if ahead:
                    raw = lax.dot_general(
                        query, piece(h_in, c, 0), LAST_WITH_LAST, preferred_element_type=F32
                    )
                    scores_in[:, base : base + keys_block] = raw
                    for j in range(0, keys_block, 128):
                        part = raw[:, j : j + 128]
                        top = part if top is None else jnp.maximum(top, part)
                if behind:
                    weights = []
                    for j in range(base, base + keys_block, 128):
                        expo = jnp.exp2(scores_out[:, j : j + 128] * EXPONENT_SCALE - shift)
                        total = expo if total is None else total + expo
                        weights.append(expo.astype(BF16))
                    part = jnp.dot(
                        jnp.concatenate(weights, axis=1),
                        piece(h_out, c, 1),
                        preferred_element_type=F32,
                    )
                    mixed = part if mixed is None else mixed + part
            if ahead:
                top_in[...] = top
            if behind:
                total = jnp.sum(total, axis=1, keepdims=True)
                result = (mixed / total).astype(BF16)
                for j in range(inner):
                    out_ref[r_out * inner + j, h_out] = result[j * tokens : (j + 1) * tokens]

        def whole(count):
            a, b = (scores_a, top_a), (scores_b, top_b)
            phase(a + (0, 0), None, count)

            def step(r, carry):
                phase(b + (1, r), a + (0, r), count)
                phase(a + (0, r + 1), b + (1, r), count)
                return carry

            lax.fori_loop(0, blocks - 1, step, 0)
            phase(b + (1, blocks - 1), a + (0, blocks - 1), count)
            phase(None, b + (1, blocks - 1), count)

        @pl.when(scalar_ref[3] > 0)
        def _():
            whole(4 * per)

        @pl.when(scalar_ref[3] == 0)
        def _():
            whole(2 * per)

    return pl.pallas_call(
        kernel,
        in_specs=[SMEM] + [VMEM] * 7,
        out_specs=VMEM,
        out_shape=jax.ShapeDtypeStruct(queries.shape, BF16),
        scratch_shapes=[
            pltpu.VMEM((rows_block, 4 * keys_each), F32),
            pltpu.VMEM((rows_block, 4 * keys_each), F32),
            pltpu.VMEM((rows_block, HEAD_DIM), F32),
            pltpu.VMEM((rows_block, HEAD_DIM), F32),
        ],
        cost_estimate=cost,
        compiler_params=pltpu.CompilerParams(vmem_limit_bytes=VMEM_LIMIT),
        name="attend",
    )(scalars, queries, *pieces)


def local(queries, keys, values, norm_gains):
    seq = lax.axis_size("seq")
    sections = lax.axis_size("section")
    here = lax.axis_index("seq")
    section = lax.axis_index("section")
    late = (section >= sections // 2).astype(jnp.int32)
    has_prior = (section > 0).astype(jnp.int32)
    scalars = jnp.stack([here // 8, here % 8 // 2, late, has_prior]).astype(jnp.int32)
    same_core = [[2 * p + c for p in range(CHIPS)] for c in range(2)]
    fence = lax.optimization_barrier

    def exchange(x):
        return lax.all_to_all(
            x, "seq", split_axis=0, concat_axis=0, tiled=True, axis_index_groups=same_core
        )

    def swap(x):
        return lax.ppermute(x, "seq", [(i, i ^ 1) for i in range(seq)])

    def passed_on(x, h):
        route = []
        for s in range(sections - 1):
            back = 8 * h if s + 1 == sections // 2 else 0
            for i in range(seq):
                route.append((s * seq + i, (s + 1) * seq + (i - back) % seq))
        return lax.ppermute(x, ("section", "seq"), route)

    own = exchange(prepare_keys_values(scalars, keys[0], values[0], norm_gains[1:2]))
    query_sent = prepare_queries(scalars, queries[0], norm_gains[0:1])
    query_sent, own = fence((query_sent, own))
    prior = [passed_on(own[:, h], h) for h in range(2)]
    head_queries = exchange(query_sent)
    own_other = swap(own)
    pieces = (own, own_other, *prior, *[swap(x) for x in prior])
    back = exchange(attend(scalars, head_queries, pieces))
    return collect(scalars, back)[None]


def solution(mesh):
    return jax.shard_map(
        local,
        mesh=mesh,
        in_specs=(
            P("section", "seq", None),
            P("section", "seq", None),
            P("section", "seq", None),
            P(),
        ),
        out_specs=P("section", "seq", None),
        check_vma=False,
    )
```

```python
import math

import jax
import jax.numpy as jnp
from jax import lax
from jax.experimental import pallas as pl
from jax.experimental.pallas import tpu as pltpu
from jax.sharding import PartitionSpec as P

HEAD_DIM = 128
RING = 4
CHIPS = RING * RING
EXPONENT_SCALE = math.log2(math.e) / math.sqrt(HEAD_DIM)
F32 = jnp.float32
BF16 = jnp.bfloat16
VMEM_LIMIT = 28 * 2**20
PREPARE_VMEM = 60 * 2**20
LAST_WITH_LAST = (((1,), (1,)), ((), ()))
VMEM = pl.BlockSpec(memory_space=pltpu.VMEM)
SMEM = pl.BlockSpec(memory_space=pltpu.SMEM)


def head_column(scalars, z, y, h):
    z = lax.rem(z + h * scalars[2], RING)
    return pl.multiple_of(((z * RING + y) * 2 + h) * HEAD_DIM, HEAD_DIM)


def norm_rows(rows, gain):
    wide = rows.astype(F32)
    power = jnp.mean(wide * wide, axis=-1, keepdims=True)
    return (wide * lax.rsqrt(power + 1e-06) * gain).astype(BF16)


def prepare(scalars, queries, keys, values, gains, rows_block=48):
    tokens, features = keys.shape

    def kernel(scalar_ref, query_ref, key_ref, value_ref, gain_ref, first_ref, second_ref, key_norm, query_norm):
        key_norm[...] = norm_rows(key_ref[...], gain_ref[1:2, :])
        query_norm[...] = norm_rows(query_ref[...], gain_ref[0:1, :])
        for c in range(CHIPS):
            for h in range(2):
                at = pl.ds(head_column(scalar_ref, c // RING, c % RING, h), HEAD_DIM)
                kv_ref = second_ref if h else first_ref
                kv_ref[c, 0] = key_norm[:, at]
                kv_ref[c, 1] = value_ref[:, at]
                first_ref[c, 2 + h] = query_norm[:, at]

    rows_spec = pl.BlockSpec((rows_block, features), lambda i, s: (i, 0))

    def out_spec(n):
        return pl.BlockSpec((CHIPS, n, rows_block, HEAD_DIM), lambda i, s: (0, 0, i, 0))

    return pl.pallas_call(
        kernel,
        grid_spec=pltpu.PrefetchScalarGridSpec(
            num_scalar_prefetch=1,
            grid=(tokens // rows_block,),
            in_specs=[rows_spec] * 3 + [pl.BlockSpec((2, features), lambda i, s: (0, 0))],
            out_specs=[out_spec(4), out_spec(2)],
            scratch_shapes=[pltpu.VMEM((rows_block, features), BF16)] * 2,
        ),
        out_shape=[
            jax.ShapeDtypeStruct((CHIPS, n, tokens, HEAD_DIM), BF16) for n in (4, 2)
        ],
        compiler_params=pltpu.CompilerParams(vmem_limit_bytes=PREPARE_VMEM),
        name="prepare",
    )(scalars, queries, keys, values, gains)


def collect(scalars, blocks):
    tokens = blocks.shape[2]

    def kernel(scalar_ref, block_ref, out_ref):
        for c in range(CHIPS):
            for h in range(2):
                column = head_column(scalar_ref, c // RING, c % RING, h)
                out_ref[:, pl.ds(column, HEAD_DIM)] = block_ref[c, h]

    return pl.pallas_call(
        kernel,
        in_specs=[SMEM, VMEM],
        out_specs=VMEM,
        out_shape=jax.ShapeDtypeStruct((tokens, CHIPS * 2 * HEAD_DIM), BF16),
        compiler_params=pltpu.CompilerParams(vmem_limit_bytes=VMEM_LIMIT),
        name="collect",
    )(scalars, blocks)


def attend(scalars, queries, h, pieces, beside=None, rows_block=192, keys_block=512):
    tokens = queries.shape[2]
    keys_each = CHIPS * tokens
    per = keys_each // keys_block
    inner = rows_block // tokens
    blocks = CHIPS // inner
    rows_all = CHIPS * tokens
    cost = pl.CostEstimate(
        flops=4 * rows_all * 4 * keys_each * HEAD_DIM,
        bytes_accessed=2 * 2 * 4 * keys_each * HEAD_DIM,
        transcendentals=rows_all * 4 * keys_each,
    )

    def kernel(scalar_ref, query_ref, *refs):
        kv = refs[:4]
        out_ref, scores_a, scores_b, top_a, top_b = refs[-5:]

        def piece(c, which):
            b, t = divmod(c, per)
            rows = kv[b][:, which].reshape(keys_each, HEAD_DIM)
            return rows[t * keys_block : (t + 1) * keys_block]

        def phase(ahead, behind, count):
            if ahead:
                scores_in, top_in, r_in = ahead
                query = jnp.concatenate(
                    [query_ref[r_in * inner + j, 2 + h] for j in range(inner)], axis=0
                )
                top = None
            if behind:
                scores_out, top_out, r_out = behind
                shift = jnp.max(top_out[...], axis=1, keepdims=True) * EXPONENT_SCALE
                shift = jnp.broadcast_to(shift, (rows_block, HEAD_DIM))
                total = None
                mixed = None
            for c in range(count):
                base = c * keys_block
                if ahead:
                    raw = lax.dot_general(
                        query, piece(c, 0), LAST_WITH_LAST, preferred_element_type=F32
                    )
                    scores_in[:, base : base + keys_block] = raw
                    for j in range(0, keys_block, 128):
                        part = raw[:, j : j + 128]
                        top = part if top is None else jnp.maximum(top, part)
                if behind:
                    weights = []
                    for j in range(base, base + keys_block, 128):
                        expo = jnp.exp2(scores_out[:, j : j + 128] * EXPONENT_SCALE - shift)
                        total = expo if total is None else total + expo
                        weights.append(expo.astype(BF16))
                    part = jnp.dot(
                        jnp.concatenate(weights, axis=1),
                        piece(c, 1),
                        preferred_element_type=F32,
                    )
                    mixed = part if mixed is None else mixed + part
            if ahead:
                top_in[...] = top
            if behind:
                total = jnp.sum(total, axis=1, keepdims=True)
                result = (mixed / total).astype(BF16)
                for j in range(inner):
                    rows = result[j * tokens : (j + 1) * tokens]
                    if beside is None:
                        out_ref[r_out * inner + j] = rows
                    else:
                        out_ref[r_out * inner + j, 0] = refs[4][r_out * inner + j]
                        out_ref[r_out * inner + j, 1] = rows

        def whole(count):
            a, b = (scores_a, top_a), (scores_b, top_b)
            phase(a + (0,), None, count)

            def step(i, carry):
                phase(b + (2 * i + 1,), a + (2 * i,), count)
                phase(a + (2 * i + 2,), b + (2 * i + 1,), count)
                return carry

            lax.fori_loop(0, blocks // 2 - 1, step, 0)
            phase(b + (blocks - 1,), a + (blocks - 2,), count)
            phase(None, b + (blocks - 1,), count)

        @pl.when(scalar_ref[3] > 0)
        def _():
            whole(4 * per)

        @pl.when(scalar_ref[3] == 0)
        def _():
            whole(2 * per)

    operands = [queries, *pieces] + ([] if beside is None else [beside])
    out_dims = (CHIPS, tokens, HEAD_DIM) if beside is None else (CHIPS, 2, tokens, HEAD_DIM)
    return pl.pallas_call(
        kernel,
        in_specs=[SMEM] + [VMEM] * len(operands),
        out_specs=VMEM,
        out_shape=jax.ShapeDtypeStruct(out_dims, BF16),
        scratch_shapes=[
            pltpu.VMEM((rows_block, 4 * keys_each), F32),
            pltpu.VMEM((rows_block, 4 * keys_each), F32),
            pltpu.VMEM((rows_block, HEAD_DIM), F32),
            pltpu.VMEM((rows_block, HEAD_DIM), F32),
        ],
        cost_estimate=cost,
        compiler_params=pltpu.CompilerParams(vmem_limit_bytes=VMEM_LIMIT),
        name="attend",
    )(scalars, *operands)


def local(queries, keys, values, norm_gains):
    seq = lax.axis_size("seq")
    sections = lax.axis_size("section")
    here = lax.axis_index("seq")
    section = lax.axis_index("section")
    late = (section >= sections // 2).astype(jnp.int32)
    has_prior = (section > 0).astype(jnp.int32)
    scalars = jnp.stack([here // 8, here % 8 // 2, late, has_prior]).astype(jnp.int32)
    same_core = [[2 * p + c for p in range(CHIPS)] for c in range(2)]
    fence = lax.optimization_barrier

    def exchange(x):
        return lax.all_to_all(
            x, "seq", split_axis=0, concat_axis=0, tiled=True, axis_index_groups=same_core
        )

    def swap(x):
        return lax.ppermute(x, "seq", [(i, i ^ 1) for i in range(seq)])

    def passed_on(x, h):
        route = []
        for s in range(sections - 1):
            back = 8 * h if s + 1 == sections // 2 else 0
            for i in range(seq):
                route.append((s * seq + i, (s + 1) * seq + (i - back) % seq))
        return lax.ppermute(x, ("section", "seq"), route)

    sent_a, sent_b = prepare(scalars, queries[0], keys[0], values[0], norm_gains)
    first = exchange(sent_a)
    sent_b, first = fence((sent_b, first))
    own_a = first[:, :2]
    prior_a = passed_on(own_a, 0)
    own_b = exchange(sent_b)
    pieces_a = [first, swap(own_a), prior_a, swap(prior_a)]
    first, own_b, pieces_a[3] = fence((first, own_b, pieces_a[3]))
    prior_b = passed_on(own_b, 1)
    out_a = attend(scalars, first, 0, pieces_a)
    own_b_other = swap(own_b)
    prior_b, out_a = fence((prior_b, out_a))
    pieces_b = [own_b, own_b_other, prior_b, swap(prior_b)]
    back = exchange(attend(scalars, first, 1, pieces_b, out_a))
    return collect(scalars, back)[None]


def solution(mesh):
    return jax.shard_map(
        local,
        mesh=mesh,
        in_specs=(
            P("section", "seq", None),
            P("section", "seq", None),
            P("section", "seq", None),
            P(),
        ),
        out_specs=P("section", "seq", None),
        check_vma=False,
    )
```
